256 devices in a mesh: tok: 8 (over y, x_hi), fin: 8 (over z), fout: 4 (over x_lo, core).
Axes of the slice: x: 4 (x_hi: 2, x_lo: 2; x = x_hi * 2 + x_lo), y: 4, z: 8, core: 2. Of those that a mesh axis runs over, the one named last changes fastest.
Arguments:
- tokens_in: bfloat16 [512, 8192], P(('tok', 'fout'), 'fin'), may hold values from -2 to 2
- cotangent: bfloat16 [512, 8192], P(('tok', 'fout'), 'fin'), may hold values from -0.19921875 to 0.19921875
- gate_weight: bfloat16 [8192, 28672], P('fin', ('tok', 'fout')), may hold values from -0.21875 to 0.21875
- up_weight: bfloat16 [8192, 28672], P('fin', ('tok', 'fout')), may hold values from -0.21875 to 0.21875
- down_weight: bfloat16 [28672, 8192], P(('tok', 'fout'), 'fin'), may hold values from -0.75 to 0.75
Outputs:
- input_grad: bfloat16 [512, 8192], P(('tok', 'fout'), 'fin')
- gate_weight_grad: bfloat16 [8192, 28672], P('fin', ('tok', 'fout'))
- up_weight_grad: bfloat16 [8192, 28672], P('fin', ('tok', 'fout'))
- down_weight_grad: bfloat16 [28672, 8192], P(('tok', 'fout'), 'fin')
The draws below stay inside these ranges and needn't reach their ends.
All inputs are finite; a program needn't handle non-finite values.
Results may differ from the reference program's by a relative error of at most 0.033.
Values may be sent and summed in bfloat16 or wider, within the bound.
A program may use at most 64 MiB of HBM per device.

```python
import jax
import jax.numpy as jnp
from jax import lax

D = 8192
FF = 28672
TOKENS = 512
BLOCK = 1024
N_FIN = 8


def levels(own_key, shape, cuts, least, top_value):
    level = 1.0
    for position, parts in cuts:
        draws = jax.random.uniform(jax.random.fold_in(jax.random.fold_in(own_key, 6), position), (parts,), jnp.float32, least / len(cuts), top_value / len(cuts))
        level = level * jnp.repeat(jnp.exp(draws), shape[position] // parts).reshape((-1,) + (1,) * (len(shape) - 1 - position))
    return level


def centred(stream_key, extent, spread, reach, cuts=(), kind=jnp.bfloat16):
    drawn = spread * jax.random.normal(stream_key, extent, jnp.float32)
    if cuts:
        drawn = drawn * levels(stream_key, extent, cuts, -0.22, 0.18)
    return jnp.clip(drawn, -reach, reach).astype(kind)


def setup_inputs(seed: int = 0) -> dict:
    seeds = jax.random.split(jax.random.key(seed), 6)
    return {
        "tokens_in": centred(seeds[0], (TOKENS, D), 0.3, 2.0, ((0, 32), (1, 8))),
        "cotangent": centred(seeds[1], (TOKENS, D), 0.03, 0.19921875, ((0, 32), (1, 8))),
        "gate_weight": centred(seeds[2], (D, FF), (D // 12) ** -0.5, 0.21875, ((0, 8), (1, 32))),
        "up_weight": centred(seeds[3], (D, FF), (D // 12) ** -0.5, 0.21875, ((0, 8), (1, 32))),
        "down_weight": centred(seeds[4], (FF, D), (D // 128) ** -0.5, 0.75, ((0, 32), (1, 8))),
    }


def block_sum(first_op, weight, weight_dim):
    def add_block(block_index, running):
        offset = (block_index * BLOCK).astype(jnp.int32)
        columns = lax.dynamic_slice_in_dim(first_op, offset, BLOCK, 1)
        weight_rows = lax.dynamic_slice_in_dim(weight, offset, BLOCK, weight_dim)
        if weight_dim == 0:
            product = jnp.dot(columns, weight_rows, preferred_element_type=jnp.float32)
        else:
            product = jnp.dot(columns, weight_rows.T, preferred_element_type=jnp.float32)
        rounded = lax.optimization_barrier(product.astype(jnp.bfloat16))
        return running + rounded.astype(jnp.float32)
    initial = jnp.zeros((first_op.shape[0], FF), jnp.float32)
    return lax.fori_loop(0, N_FIN, add_block, initial)


def activations(gate_sum, up_sum, hidden_grad):
    sigmoid_gate = jax.nn.sigmoid(gate_sum)
    silu_gate = gate_sum * sigmoid_gate
    hidden = (silu_gate * up_sum).astype(jnp.bfloat16)
    gate_grad = (hidden_grad * up_sum * sigmoid_gate * (1.0 + gate_sum * (1.0 - sigmoid_gate))).astype(jnp.bfloat16)
    up_grad = (hidden_grad * silu_gate).astype(jnp.bfloat16)
    return hidden, gate_grad, up_grad


def outer_grads(first_op, second_op):
    width = first_op.shape[1]
    pieces = first_op.reshape(first_op.shape[0], 8, width // 8).transpose(1, 0, 2)
    result = lax.map(lambda block_rows: jnp.dot(block_rows.T, second_op, preferred_element_type=jnp.float32).astype(jnp.bfloat16), pieces)
    return result.reshape(width, second_op.shape[1])


def reference(tokens_in, cotangent, gate_weight, up_weight, down_weight):
    gate_sum = block_sum(tokens_in, gate_weight, 0)
    up_sum = block_sum(tokens_in, up_weight, 0)
    hidden_grad = block_sum(cotangent, down_weight, 1)
    hidden, gate_grad, up_grad = activations(gate_sum, up_sum, hidden_grad)
    down_weight_grad = outer_grads(hidden, cotangent)
    gate_weight_grad = outer_grads(tokens_in, gate_grad)
    up_weight_grad = outer_grads(tokens_in, up_grad)
    dims = (((1,), (1,)), ((), ()))
    input_sum = lax.dot_general(gate_grad, gate_weight, dims, preferred_element_type=jnp.float32)
    input_sum = input_sum + lax.dot_general(up_grad, up_weight, dims, preferred_element_type=jnp.float32)
    return input_sum.astype(jnp.bfloat16), gate_weight_grad, up_weight_grad, down_weight_grad
```

```python
import functools

import jax
import jax.numpy as jnp
from jax import lax
from jax.experimental import pallas as pl
from jax.experimental.pallas import tpu as pltpu
from jax.sharding import PartitionSpec as P

MESH = pl.DeviceIdType.MESH
BF = jnp.bfloat16
F32 = jnp.float32
NT = (((1,), (1,)), ((), ()))
DY = (0, 1, 3, 2)
DX = (1, 3, 2)
NZ = 8
NR = 4


def kernel(
    x_hbm, ct_hbm, wg_hbm, wu_hbm, wd_hbm,
    ig_out, dwg_out, dwu_out, dwd_out,
    xb, xt, wg, wu, wd, pt, sdn, sup, rdn, rup, gb, acc, igs, igr, iys, iyr, igacc,
    w_sem, xs_sem, xr_sem, ys_sem, yr_sem, cs_sem, cr_sem,
    rs_s, rs_r, ag_s, ag_r, is_s, is_r, iy_s, iy_r,
):
    tok, z, fout = lax.axis_index("tok"), lax.axis_index("fin"), lax.axis_index("fout")
    y, x = tok // 2, (tok % 2) * 2 + fout // 2
    core = fout % 2
    me = x * 2 + core

    def at(y_, x_, c_, z_):
        return dict(tok=y_ * 2 + x_ // 2, fin=z_, fout=(x_ % 2) * 2 + c_)

    def row_peer(k):
        j = (me + k) % 8
        return at(y, j // 2, j % 2, z)

    partner = at(y, x, 1 - core, z)
    xpeer = [at(y, (x + d) % 4, core, z) for d in DX]
    ypeer = [None] + [at((y + d) % 4, x, core, z) for d in DY[1:]]
    zdn = at(y, x, core, (z + NZ - 1) % NZ)
    zup = at(y, x, core, (z + 1) % NZ)

    def rcopy(src, dst, ss, rs, dev):
        return pltpu.make_async_remote_copy(
            src_ref=src, dst_ref=dst, send_sem=ss, recv_sem=rs, device_id=dev, device_id_type=MESH
        )

    sends = []

    def start(copy):
        copy.start()
        sends.append(copy)

    loads = [
        pltpu.make_async_copy(x_hbm, xb.at[0, me, 0], w_sem.at[0]),
        pltpu.make_async_copy(ct_hbm, xb.at[0, me, 1], w_sem.at[1]),
        pltpu.make_async_copy(wg_hbm, wg, w_sem.at[2]),
        pltpu.make_async_copy(wu_hbm, wu, w_sem.at[3]),
        pltpu.make_async_copy(wd_hbm, wd, w_sem.at[4]),
    ]
    for c in loads:
        c.start()

    bar = pltpu.get_barrier_semaphore()
    everyone = [row_peer(k) for k in range(1, 8)] + ypeer[1:] + [zdn, zup]
    for p in everyone:
        pl.semaphore_signal(bar, inc=1, device_id=p, device_id_type=MESH)
    pl.semaphore_wait(bar, len(everyone))

    loads[0].wait()
    loads[1].wait()

    def x_copy(i):
        return rcopy(xb.at[0, me], xb.at[0, me], xs_sem.at[i], xr_sem.at[i], xpeer[i])

    def blk(k):
        return me if k == 0 else ((x + DX[k - 1]) % 4) * 2 + core

    REV = {1: 3, 3: 1, 2: 2}

    def y_copy(r, k):
        rr = DY.index((4 - DY[r]) % 4)
        return rcopy(xb.at[0, blk(k)], xb.at[rr, blk(k)], ys_sem.at[r, k], yr_sem.at[rr, k], ypeer[r])

    def c_copy(r, k):
        return rcopy(xb.at[r, blk(k)], xb.at[r, blk(k)], cs_sem.at[r, k], cr_sem.at[r, k], partner)

    def x_recv(i):
        n = DX.index(REV[DX[i]])
        return rcopy(xb.at[0, blk(i + 1)], xb.at[0, blk(i + 1)], xs_sem.at[n], xr_sem.at[n], xpeer[i])

    def y_recv(r, k):
        return rcopy(xb.at[r, blk(k)], xb.at[r, blk(k)], ys_sem.at[r, k], yr_sem.at[r, k], ypeer[r])

    def c_recv(r, k):
        b = blk(k) + 1 - 2 * core
        return rcopy(xb.at[r, b], xb.at[r, b], cs_sem.at[r, k], cr_sem.at[r, k], partner)

    for i in range(3):
        start(x_copy(i))
    start(c_copy(0, 0))
    for r in (1, 2):
        start(y_copy(r, 0))
    for i in range(3):
        x_recv(i).wait_recv()
        start(c_copy(0, i + 1))
        for r in (1, 2):
            start(y_copy(r, i + 1))
    for k in range(4):
        start(y_copy(3, k))

    def gather_done(r):
        if r > 0:
            for k in range(4):
                y_recv(r, k).wait_recv()
                start(c_copy(r, k))
        for k in range(4):
            c_recv(r, k).wait_recv()

    nd = [4, 3, 4, 3]

    def partials(r):
        gather_done(r)
        if r == 0:
            for c in loads[2:]:
                c.wait()
        toks = xb[r, :, 0].reshape(128, 1024)
        cots = xb[r, :, 1].reshape(128, 1024)
        pt[r, :, 0] = jnp.dot(toks, wg[...], preferred_element_type=F32).reshape(8, 16, 896)
        pt[r, :, 1] = jnp.dot(toks, wu[...], preferred_element_type=F32).reshape(8, 16, 896)
        pt[r, :, 2] = lax.dot_general(cots, wd[...], NT, preferred_element_type=F32).reshape(8, 16, 896)
        send_sums(r, 0)
        xt[r] = toks.T

    def dn_copy(r, s):
        return rcopy(sdn.at[r, s], rdn.at[r, s], rs_s.at[r, 0, s], rs_r.at[r, 0, s], zdn)

    def up_copy(r, s):
        return rcopy(sup.at[r, s], rup.at[r, s], rs_s.at[r, 1, s], rs_r.at[r, 1, s], zup)

    def send_sums(r, s):
        n, m = nd[r], 7 - nd[r]
        if s < n:
            mine = pt[r, (z - n + s + NZ) % NZ]
            if s > 0:
                dn_copy(r, s - 1).wait_recv()
                mine = mine + rdn[r, s - 1].astype(F32)
            sdn[r, s] = mine.astype(BF)
            start(dn_copy(r, s))
        if s < m:
            mine = pt[r, (z + m - s) % NZ]
            if s > 0:
                up_copy(r, s - 1).wait_recv()
                mine = mine + rup[r, s - 1].astype(F32)
            sup[r, s] = mine.astype(BF)
            start(up_copy(r, s))

    def ag_copy(r, d, t):
        c = (z + t) % NZ if d == 0 else (z - t + NZ) % NZ
        return rcopy(gb.at[r, c], gb.at[r, c], ag_s.at[r, d, t], ag_r.at[r, d, t], zdn if d == 0 else zup)

    def ag_recv(r, d, t):
        c = (z + t + 1) % NZ if d == 0 else (z - t - 1 + NZ) % NZ
        return rcopy(gb.at[r, c], gb.at[r, c], ag_s.at[r, d, t], ag_r.at[r, d, t], zdn if d == 0 else zup)

    def act(r):
        n, m = nd[r], 7 - nd[r]
        dn_copy(r, n - 1).wait_recv()
        up_copy(r, m - 1).wait_recv()
        total = pt[r, z] + rdn[r, n - 1].astype(F32) + rup[r, m - 1].astype(F32)
        g, u, hg = total[0], total[1], total[2]
        s = jax.nn.sigmoid(g)
        silu = g * s
        gb[r, z, 0] = (silu * u).astype(BF)
        gb[r, z, 1] = (hg * u * s * (1.0 + g * (1.0 - s))).astype(BF)
        gb[r, z, 2] = (hg * silu).astype(BF)

    def spread(r, t):
        hops = (7 - nd[r], nd[r])
        for d in (0, 1):
            if t > 0 and t <= hops[d]:
                ag_recv(r, d, t - 1).wait_recv()
            if t < hops[d]:
                start(ag_copy(r, d, t))

    def stage(r, s):
        if s < 4:
            send_sums(r, s)
        elif s == 4:
            act(r)
            spread(r, 0)
        else:
            spread(r, s - 4)

    def ig_copy(r, k):
        j = (me + k) % 8
        return rcopy(igs.at[r, j], igr.at[r, 8 - k], is_s.at[r, k], is_r.at[r, 8 - k], row_peer(k))

    def ig_recv(r, k):
        return rcopy(igs.at[r, 0], igr.at[r, k], is_s.at[r, k], is_r.at[r, k], row_peer(k))

    def input_part(r):
        gg = gb[r, :, 1].reshape(128, 896)
        ug = gb[r, :, 2].reshape(128, 896)
        part = lax.dot_general(gg, wg[...], NT, preferred_element_type=F32)
        part = part + lax.dot_general(ug, wu[...], NT, preferred_element_type=F32)
        igs[r] = part.astype(BF).reshape(8, 16, 1024)
        for k in range(1, 8):
            start(ig_copy(r, k))

    def add_dw(r, i, lhs_t, rhs, out, rows):
        step = 128
        def body(m, _):
            sl = pl.ds(pl.multiple_of(m * step, step), step)
            v = jnp.dot(lhs_t[sl, :], rhs, preferred_element_type=F32)
            if r > 0:
                v = v + acc[i, sl, :rhs.shape[1]]
            if r < NR - 1:
                acc[i, sl, :rhs.shape[1]] = v
            else:
                out[sl, :] = v.astype(BF)
            return 0
        lax.fori_loop(0, rows // step, body, 0)

    def dw_gate(r):
        add_dw(r, 0, xt.at[r], gb[r, :, 1].reshape(128, 896), dwg_out, 1024)

    def dw_up(r):
        add_dw(r, 1, xt.at[r], gb[r, :, 2].reshape(128, 896), dwu_out, 1024)

    def dw_down(r):
        xt[r, :896] = gb[r, :, 0].reshape(128, 896).T
        add_dw(r, 2, xt.at[r], xb[r, :, 1].reshape(128, 1024), dwd_out, 896)

    def iy_copy(r):
        return rcopy(iys.at[r], iyr.at[r], iy_s.at[r], iy_r.at[r], ypeer[r])

    def row_sum(r):
        for k in range(1, 8):
            ig_recv(r, k).wait_recv()
        v = igs[r, me].astype(F32)
        for k in range(1, 8):
            v = v + igr[r, k].astype(F32)
        if r == 0:
            igacc[...] = v
        else:
            iys[r] = v.astype(BF)
            start(iy_copy(r))

    partials(0)
    stage(0, 1)
    partials(1)
    partials(2)
    stage(0, 2)
    stage(1, 1)
    stage(2, 1)
    partials(3)
    done = [2, 1, 1, 0]
    while min(done) < 8:
        for r in range(4):
            if done[r] < 8:
                done[r] += 1
                stage(r, done[r])
                if done[r] == 8:
                    input_part(r)
                    dw_gate(r)
                    dw_up(r)
                    if r > 0:
                        row_sum(r - 1)
                    dw_down(r)
    row_sum(3)
    total = igacc[...]
    for r in range(1, 4):
        iy_copy(r).wait_recv()
        total = total + iyr[r].astype(F32)
    ig_out[...] = total.astype(BF)
    for c in sends:
        c.wait_send()


def local(tokens_in, cotangent, gate_weight, up_weight, down_weight):
    vm = pltpu.VMEM
    dma = pltpu.SemaphoreType.DMA
    return pl.pallas_call(
        kernel,
        out_shape=(
            jax.ShapeDtypeStruct((16, 1024), BF),
            jax.ShapeDtypeStruct((1024, 896), BF),
            jax.ShapeDtypeStruct((1024, 896), BF),
            jax.ShapeDtypeStruct((896, 1024), BF),
        ),
        in_specs=[pl.BlockSpec(memory_space=pl.ANY)] * 5,
        out_specs=[pl.BlockSpec(memory_space=pltpu.VMEM)] * 4,
        scratch_shapes=[
            vm((4, 8, 2, 16, 1024), BF),
            vm((4, 1024, 128), BF),
            vm((1024, 896), BF),
            vm((1024, 896), BF),
            vm((896, 1024), BF),
            vm((4, 8, 3, 16, 896), F32),
            vm((4, 4, 3, 16, 896), BF),
            vm((4, 4, 3, 16, 896), BF),
            vm((4, 4, 3, 16, 896), BF),
            vm((4, 4, 3, 16, 896), BF),
            vm((4, 8, 3, 16, 896), BF),
            vm((3, 1024, 1024), F32),
            vm((4, 8, 16, 1024), BF),
            vm((4, 8, 16, 1024), BF),
            vm((4, 16, 1024), BF),
            vm((4, 16, 1024), BF),
            vm((16, 1024), F32),
            dma((5,)),
            dma((3,)), dma((3,)),
            dma((4, 4)), dma((4, 4)),
            dma((4, 4)), dma((4, 4)),
            dma((4, 2, 4)), dma((4, 2, 4)),
            dma((4, 2, 4)), dma((4, 2, 4)),
            dma((4, 8)), dma((4, 8)),
            dma((4,)), dma((4,)),
        ],
        compiler_params=pltpu.CompilerParams(
            collective_id=0, has_side_effects=True, vmem_limit_bytes=56 * 2**20
        ),
        cost_estimate=pl.CostEstimate(flops=7_516_000_000, bytes_accessed=11_000_000, transcendentals=0),
    )(tokens_in, cotangent, gate_weight, up_weight, down_weight)


def solution(mesh):
    in_specs = (
        P(("tok", "fout"), "fin"),
        P(("tok", "fout"), "fin"),
        P("fin", ("tok", "fout")),
        P("fin", ("tok", "fout")),
        P(("tok", "fout"), "fin"),
    )
    out_specs = (
        P(("tok", "fout"), "fin"),
        P("fin", ("tok", "fout")),
        P("fin", ("tok", "fout")),
        P(("tok", "fout"), "fin"),
    )
    return jax.shard_map(local, mesh=mesh, in_specs=in_specs, out_specs=out_specs, check_vma=False)
```

```python
import functools

import jax
import jax.numpy as jnp
from jax import lax
from jax.experimental import pallas as pl
from jax.experimental.pallas import tpu as pltpu
from jax.sharding import PartitionSpec as P

MESH = pl.DeviceIdType.MESH
BF = jnp.bfloat16
F32 = jnp.float32
NT = (((1,), (1,)), ((), ()))
DY = (0, 1, 3, 2)
DX = (1, 3, 2)
NZ = 8
NR = 4


def kernel(
    x_hbm, ct_hbm, wg_hbm, wu_hbm, wd_hbm,
    ig_out, dwg_out, dwu_out, dwd_out,
    xb, xt, ht, wgu, wd, pt, sdn, sup, rdn, rup, gb, acc, igs, igr, ips, ipr, ilr, iys, iyr, igacc,
    w_sem, tx_s, tx_r, ty_s, ty_r, ox_s, ox_r, oy_s, oy_r, c0_s, c0_r, cc_s, cc_r,
    rs_s, rs_r, ag_s, ag_r, is_s, is_r, i0_s, i0_r, ix_s, ix_r, il_s, il_r, iy_s, iy_r,
):
    tok, z, fout = lax.axis_index("tok"), lax.axis_index("fin"), lax.axis_index("fout")
    y, x = tok // 2, (tok % 2) * 2 + fout // 2
    core = fout % 2
    me = core * 4 + x

    def at(y_, x_, c_, z_):
        return dict(tok=y_ * 2 + x_ // 2, fin=z_, fout=(x_ % 2) * 2 + c_)

    def row_peer(k):
        j = (me + k) % 8
        return at(y, j % 4, j // 4, z)

    partner = at(y, x, 1 - core, z)
    xpeer = [at(y, (x + d) % 4, core, z) for d in DX]
    ypeer = [None] + [at((y + d) % 4, x, core, z) for d in DY[1:]]
    zdn = at(y, x, core, (z + NZ - 1) % NZ)
    zup = at(y, x, core, (z + 1) % NZ)
    BACK = (0, 2, 1, 3)

    def rcopy(src, dst, ss, rs, dev):
        return pltpu.make_async_remote_copy(
            src_ref=src, dst_ref=dst, send_sem=ss, recv_sem=rs, device_id=dev, device_id_type=MESH
        )

    sends = []

    def start(copy):
        copy.start()
        sends.append(copy)

    loads = [
        pltpu.make_async_copy(x_hbm, xb.at[0, 0, me], w_sem.at[0]),
        pltpu.make_async_copy(ct_hbm, xb.at[0, 1, me], w_sem.at[1]),
        pltpu.make_async_copy(wg_hbm, wgu.at[:, 0:896], w_sem.at[2]),
        pltpu.make_async_copy(wu_hbm, wgu.at[:, 896:1792], w_sem.at[3]),
        pltpu.make_async_copy(wd_hbm, wd, w_sem.at[4]),
    ]
    for c in loads:
        c.start()

    bar = pltpu.get_barrier_semaphore()
    everyone = [row_peer(k) for k in range(1, 8)] + ypeer[1:] + [zdn, zup]
    for p in everyone:
        pl.semaphore_signal(bar, inc=1, device_id=p, device_id_type=MESH)
    pl.semaphore_wait(bar, len(everyone))

    def blk(k):
        return core * 4 + (x if k == 0 else (x + DX[k - 1]) % 4)

    def tx_send(r, i):
        return rcopy(xb.at[r, 0, me], xb.at[r, 0, me], tx_s.at[r, i], tx_r.at[r, i], xpeer[i])

    def tx_recv(r, k):
        n = BACK[k] - 1
        return rcopy(xb.at[r, 0, blk(k)], xb.at[r, 0, blk(k)], tx_s.at[r, n], tx_r.at[r, n], xpeer[k - 1])

    def ty_send(r):
        return rcopy(xb.at[0, 0, me], xb.at[BACK[r], 0, me], ty_s.at[r], ty_r.at[BACK[r]], ypeer[r])

    def ty_recv(r):
        return rcopy(xb.at[r, 0, me], xb.at[r, 0, me], ty_s.at[r], ty_r.at[r], ypeer[r])

    def ox_send(i):
        return rcopy(xb.at[0, 1, me], xb.at[0, 1, me], ox_s.at[i], ox_r.at[i], xpeer[i])

    def ox_recv(k):
        n = BACK[k] - 1
        return rcopy(xb.at[0, 1, blk(k)], xb.at[0, 1, blk(k)], ox_s.at[n], ox_r.at[n], xpeer[k - 1])

    def oy_send(r, k):
        q = BACK[r]
        return rcopy(xb.at[0, 1, blk(k)], xb.at[q, 1, blk(k)], oy_s.at[r, k], oy_r.at[q, k], ypeer[r])

    def oy_recv(r, k):
        return rcopy(xb.at[r, 1, blk(k)], xb.at[r, 1, blk(k)], oy_s.at[r, k], oy_r.at[r, k], ypeer[r])

    def c0_copy(a, k, own=True):
        b = blk(k) if own else (4 - 4 * core) + blk(k) - 4 * core
        return rcopy(xb.at[0, a, b], xb.at[0, a, b], c0_s.at[a, k], c0_r.at[a, k], partner)

    def cc_copy(r, a, own=True):
        b = pl.ds(4 * core if own else 4 - 4 * core, 4)
        return rcopy(xb.at[r, a, b], xb.at[r, a, b], cc_s.at[r, a], cc_r.at[r, a], partner)

    def own_sends():
        loads[0].wait()
        for i in range(3):
            start(tx_send(0, i))
        start(c0_copy(0, 0))
        start(ty_send(1))
        loads[1].wait()
        for i in range(3):
            start(ox_send(i))
        start(c0_copy(1, 0))
        start(oy_send(1, 0))
        start(ty_send(2))
        start(oy_send(2, 0))

    def tok_in():
        for k in (1, 2, 3):
            tx_recv(0, k).wait_recv()
            start(c0_copy(0, k))

    def forward_y(r):
        ty_recv(r).wait_recv()
        for i in range(3):
            start(tx_send(r, i))

    def cot_in():
        for k in (1, 2, 3):
            ox_recv(k).wait_recv()
            start(c0_copy(1, k))
            start(oy_send(1, k))

    def send_y(r):
        if r == 2:
            for k in (1, 2, 3):
                start(oy_send(2, k))
        else:
            start(ty_send(3))
            for k in range(4):
                start(oy_send(3, k))

    nd = [4, 3, 4, 3]

    def hand_over(r):
        for k in (1, 2, 3):
            tx_recv(r, k).wait_recv()
        start(cc_copy(r, 0))
        for k in (0, 1, 2, 3):
            oy_recv(r, k).wait_recv()
        start(cc_copy(r, 1))

    def partials(r):
        if r == 0:
            for k in range(4):
                c0_copy(0, k, False).wait_recv()
            loads[2].wait()
            loads[3].wait()
        else:
            cc_copy(r, 0, False).wait_recv()
        toks = xb[r, 0].reshape(128, 1024)
        both = jnp.dot(toks, wgu[...], preferred_element_type=F32)
        pt[r, :, 0] = both[:, :896].reshape(8, 16, 896)
        pt[r, :, 1] = both[:, 896:].reshape(8, 16, 896)
        if r == 0:
            for k in range(4):
                c0_copy(1, k, False).wait_recv()
            loads[4].wait()
        else:
            cc_copy(r, 1, False).wait_recv()
        cots = xb[r, 1].reshape(128, 1024)
        pt[r, :, 2] = lax.dot_general(cots, wd[...], NT, preferred_element_type=F32).reshape(8, 16, 896)
        send_sums(r, 0)
        xt[r // 2, :, (r % 2) * 128:(r % 2) * 128 + 128] = toks.T

    def dn_copy(r, s):
        return rcopy(sdn.at[r, s], rdn.at[r, s], rs_s.at[r, 0, s], rs_r.at[r, 0, s], zdn)

    def up_copy(r, s):
        return rcopy(sup.at[r, s], rup.at[r, s], rs_s.at[r, 1, s], rs_r.at[r, 1, s], zup)

    def send_sums(r, s):
        n, m = nd[r], 7 - nd[r]
        if s < n:
            mine = pt[r, (z - n + s + NZ) % NZ]
            if s > 0:
                dn_copy(r, s - 1).wait_recv()
                mine = mine + rdn[r, s - 1].astype(F32)
            sdn[r, s] = mine.astype(BF)
            start(dn_copy(r, s))
        if s < m:
            mine = pt[r, (z + m - s) % NZ]
            if s > 0:
                up_copy(r, s - 1).wait_recv()
                mine = mine + rup[r, s - 1].astype(F32)
            sup[r, s] = mine.astype(BF)
            start(up_copy(r, s))

    def ag_copy(r, d, t, recv=False):
        t_ = t + 1 if recv else t
        c = (z + t_) % NZ if d == 0 else (z - t_ + NZ) % NZ
        return rcopy(gb.at[r, c], gb.at[r, c], ag_s.at[r, d, t], ag_r.at[r, d, t], zdn if d == 0 else zup)

    def act(r):
        n, m = nd[r], 7 - nd[r]
        dn_copy(r, n - 1).wait_recv()
        up_copy(r, m - 1).wait_recv()
        total = pt[r, z] + rdn[r, n - 1].astype(F32) + rup[r, m - 1].astype(F32)
        g, u, hg = total[0], total[1], total[2]
        s = jax.nn.sigmoid(g)
        silu = g * s
        gb[r, z, 2] = (silu * u).astype(BF)
        gb[r, z, 0] = (hg * u * s * (1.0 + g * (1.0 - s))).astype(BF)
        gb[r, z, 1] = (hg * silu).astype(BF)

    def spread(r, t):
        hops = (7 - nd[r], nd[r])
        for d in (0, 1):
            if 0 < t <= hops[d]:
                ag_copy(r, d, t - 1, True).wait_recv()
            if t < hops[d]:
                start(ag_copy(r, d, t))

    def stage(r, s):
        if s < 4:
            send_sums(r, s)
        else:
            if s == 4:
                act(r)
            spread(r, s - 4)

    def pr_copy(r):
        b = pl.ds(4 - 4 * core, 4)
        return rcopy(igs.at[r, b], igr.at[r], is_s.at[r], is_r.at[r], partner)

    def p0_copy(i):
        return rcopy(igs.at[0, 4 - 4 * core + i], igr.at[0, i], i0_s.at[i], i0_r.at[i], partner)

    def px_copy(r, n):
        m = BACK[n + 1] - 1
        return rcopy(ips.at[r, (x + DX[n]) % 4], ipr.at[r, m], ix_s.at[r, n], ix_r.at[r, m], xpeer[n])

    def px_recv(r, n):
        return rcopy(ips.at[r, 0], ipr.at[r, n], ix_s.at[r, n], ix_r.at[r, n], xpeer[n])

    far = (z + 4) % NZ

    def late_copy():
        n = (me - far + 8) % 8
        return rcopy(igs.at[0, far], ilr.at[n], il_s.at[0], il_r.at[n], at(y, far % 4, far // 4, z))

    def late_recv(n):
        return rcopy(igs.at[0, 0], ilr.at[n], il_s.at[0], il_r.at[n], row_peer(n))

    def input_rows(r, chunks):
        both = jnp.concatenate(
            [jnp.concatenate([gb[r, c, 0], gb[r, c, 1]], axis=1) for c in chunks], axis=0
        )
        part = lax.dot_general(both, wgu[...], NT, preferred_element_type=F32).astype(BF)
        for n, c in enumerate(chunks):
            igs[r, c] = part[16 * n:16 * n + 16]

    def input_part(r):
        input_rows(r, range(8))
        start(pr_copy(r))

    def pair_sum(r):
        pr_copy(r).wait_recv()
        own = igs[r, pl.ds(4 * core, 4)]
        ips[r] = (own.astype(F32) + igr[r].astype(F32)).astype(BF)
        for n in range(3):
            start(px_copy(r, n))

    def input_early():
        input_rows(0, [(z + n + NZ) % NZ for n in range(-3, 4)])
        for i in range(4):

            @pl.when(4 - 4 * core + i != far)
            def _(i=i):
                p0_copy(i).start()

    def pair_early():
        for n in range(4):
            i = (x + ((0,) + DX)[n]) % 4

            @pl.when(4 * core + i != far)
            def _(i=i, n=n):
                p0_copy(i).wait_recv()
                own = igs[0, 4 * core + i]
                ips[0, i] = (own.astype(F32) + igr[0, i].astype(F32)).astype(BF)
                if n > 0:
                    px_copy(0, n - 1).start()

    def input_late():
        input_rows(0, [far])

        @pl.when(me != far)
        def _():
            late_copy().start()

    def add_dw(p, i, lhs, rhs, out, first):
        width = rhs.shape[1]
        for c in range(0, width, 256):
            e = min(c + 256, width)
            v = jnp.dot(lhs, rhs[:, c:e], preferred_element_type=F32)
            if first:
                acc[i, :lhs.shape[0], c:e] = v
            else:
                out[:, c:e] = (acc[i, :lhs.shape[0], c:e] + v).astype(BF)

    def weights_part(p, first):
        rs = slice(2 * p, 2 * p + 2)
        add_dw(p, 0, xt[p], gb[rs, :, 0].reshape(256, 896), dwg_out, first)
        add_dw(p, 1, xt[p], gb[rs, :, 1].reshape(256, 896), dwu_out, first)
        ht[...] = gb[rs, :, 2].reshape(256, 896).T
        add_dw(p, 2, ht[...], xb[rs, 1].reshape(256, 1024), dwd_out, first)

    def iy_copy(r):
        return rcopy(iys.at[r], iyr.at[r], iy_s.at[r], iy_r.at[r], ypeer[r])

    def row_sum(r):
        v = ips[r, x].astype(F32)
        for n in range(3):
            px_recv(r, n).wait_recv()
            v = v + ipr[r, n].astype(F32)
        iys[r] = v.astype(BF)
        start(iy_copy(r))

    def finish():
        @pl.when(me != far)
        def _():
            v = ips[0, x].astype(F32)
            for n in range(3):
                px_recv(0, n).wait_recv()
                v = v + ipr[0, n].astype(F32)
            igacc[...] = v

        @pl.when(me == far)
        def _():
            v = igs[0, me].astype(F32)
            for n in range(1, 8):
                late_recv(n).wait_recv()
                v = v + ilr[n].astype(F32)
            igacc[...] = v

        total = igacc[...]
        for r in (1, 2, 3):
            iy_copy(r).wait_recv()
            total = total + iyr[r].astype(F32)
        ig_out[...] = total.astype(BF)
        for i in range(4):

            @pl.when(4 - 4 * core + i != far)
            def _(i=i):
                p0_copy(i).wait_send()

        for n in range(3):

            @pl.when(4 * core + (x + DX[n]) % 4 != far)
            def _(n=n):
                px_copy(0, n).wait_send()

        @pl.when(me != far)
        def _():
            late_copy().wait_send()

    steps = []

    def then(fn, *given):
        steps.append((fn, given))

    then(own_sends)
    then(tok_in)
    then(forward_y, 1)
    then(cot_in)
    then(partials, 0)
    then(forward_y, 2)
    then(send_y, 2)
    then(hand_over, 1)
    then(partials, 1)
    then(send_y, 3)
    then(hand_over, 2)
    then(stage, 0, 1)
    then(partials, 2)
    then(stage, 1, 1)
    then(forward_y, 3)
    then(stage, 0, 2)
    then(stage, 2, 1)
    then(hand_over, 3)
    then(stage, 1, 2)
    then(partials, 3)
    for s in range(3, 9):
        then(stage, 1, s)
        then(stage, 2, s - 1)
        then(stage, 3, s - 2)
        if s > 5:
            then(stage, 0, s - 3)
    then(input_part, 1)
    then(stage, 2, 8)
    then(stage, 3, 7)
    then(stage, 0, 6)
    then(input_part, 2)
    then(pair_sum, 1)
    then(stage, 0, 7)
    then(stage, 3, 8)
    then(input_part, 3)
    then(pair_sum, 2)
    then(input_early)
    then(row_sum, 1)
    then(pair_sum, 3)
    then(row_sum, 2)
    then(pair_early)
    then(weights_part, 1, True)
    then(stage, 0, 8)
    then(input_late)
    then(row_sum, 3)
    then(weights_part, 0, False)
    then(finish)
    for fn, given in steps:
        fn(*given)
    for c in sends:
        c.wait_send()


def writer(*refs):
    sem = refs[8]
    copies = [pltpu.make_async_copy(refs[i], refs[4 + i], sem.at[i]) for i in range(4)]
    for c in copies:
        c.start()
    for c in copies:
        c.wait()


def local(tokens_in, cotangent, gate_weight, up_weight, down_weight):
    vm = pltpu.VMEM
    dma = pltpu.SemaphoreType.DMA
    outs = pl.pallas_call(
        kernel,
        out_shape=(
            pltpu.VMEM((16, 1024), BF),
            pltpu.VMEM((1024, 896), BF),
            pltpu.VMEM((1024, 896), BF),
            pltpu.VMEM((896, 1024), BF),
        ),
        in_specs=[pl.BlockSpec(memory_space=pl.ANY)] * 5,
        out_specs=[pl.BlockSpec(memory_space=pltpu.VMEM)] * 4,
        scratch_shapes=[
            vm((4, 2, 8, 16, 1024), BF),
            vm((2, 1024, 256), BF),
            vm((896, 256), BF),
            vm((1024, 1792), BF),
            vm((896, 1024), BF),
            vm((4, 8, 3, 16, 896), F32),
            vm((4, 4, 3, 16, 896), BF),
            vm((4, 4, 3, 16, 896), BF),
            vm((4, 4, 3, 16, 896), BF),
            vm((4, 4, 3, 16, 896), BF),
            vm((4, 8, 3, 16, 896), BF),
            vm((3, 1024, 1024), F32),
            vm((4, 8, 16, 1024), BF),
            vm((4, 4, 16, 1024), BF),
            vm((4, 4, 16, 1024), BF),
            vm((4, 3, 16, 1024), BF),
            vm((8, 16, 1024), BF),
            vm((4, 16, 1024), BF),
            vm((4, 16, 1024), BF),
            vm((16, 1024), F32),
            dma((5,)),
            dma((4, 3)), dma((4, 3)),
            dma((4,)), dma((4,)),
            dma((3,)), dma((3,)),
            dma((4, 4)), dma((4, 4)),
            dma((2, 4)), dma((2, 4)),
            dma((4, 2)), dma((4, 2)),
            dma((4, 2, 4)), dma((4, 2, 4)),
            dma((4, 2, 4)), dma((4, 2, 4)),
            dma((4,)), dma((4,)),
            dma((4,)), dma((4,)),
            dma((4, 3)), dma((4, 3)),
            dma((1,)), dma((8,)),
            dma((4,)), dma((4,)),
        ],
        compiler_params=pltpu.CompilerParams(
            collective_id=0, has_side_effects=True, vmem_limit_bytes=48 * 2**20
        ),
        cost_estimate=pl.CostEstimate(flops=7_516_000_000, bytes_accessed=11_000_000, transcendentals=0),
    )(tokens_in, cotangent, gate_weight, up_weight, down_weight)
    outs = [pltpu.with_memory_space_constraint(a, pltpu.MemorySpace.VMEM) for a in outs]
    return pl.pallas_call(
        writer,
        out_shape=(
            jax.ShapeDtypeStruct((16, 1024), BF),
            jax.ShapeDtypeStruct((1024, 896), BF),
            jax.ShapeDtypeStruct((1024, 896), BF),
            jax.ShapeDtypeStruct((896, 1024), BF),
        ),
        in_specs=[pl.BlockSpec(memory_space=pltpu.VMEM)] * 4,
        out_specs=[pl.BlockSpec(memory_space=pl.ANY)] * 4,
        scratch_shapes=[pltpu.SemaphoreType.DMA((4,))],
        compiler_params=pltpu.CompilerParams(vmem_limit_bytes=2**20),
        cost_estimate=pl.CostEstimate(flops=0, bytes_accessed=11_000_000, transcendentals=0),
    )(*outs)


def solution(mesh):
    in_specs = (
        P(("tok", "fout"), "fin"),
        P(("tok", "fout"), "fin"),
        P("fin", ("tok", "fout")),
        P("fin", ("tok", "fout")),
        P(("tok", "fout"), "fin"),
    )
    out_specs = (
        P(("tok", "fout"), "fin"),
        P("fin", ("tok", "fout")),
        P("fin", ("tok", "fout")),
        P(("tok", "fout"), "fin"),
    )
    return jax.shard_map(local, mesh=mesh, in_specs=in_specs, out_specs=out_specs, check_vma=False)
```

```python
import functools

import jax
import jax.numpy as jnp
from jax import lax
from jax.experimental import pallas as pl
from jax.experimental.pallas import tpu as pltpu
from jax.sharding import PartitionSpec as P

MESH = pl.DeviceIdType.MESH
BF = jnp.bfloat16
F32 = jnp.float32
NT = (((1,), (1,)), ((), ()))
DY = (0, 1, 3, 2)
DX = (1, 3, 2)
NZ = 8
NR = 4


def kernel(
    x_hbm, ct_hbm, wg_hbm, wu_hbm, wd_hbm,
    ig_out, dwg_out, dwu_out, dwd_out,
    xb, xt, ht, wgu, wd, pt, sdn, sup, rdn, rup, gb, igs, igr, ips, ipr, ils, ilr, iys, iyr, igacc,
    w_sem, g_s, g_r, c0_s, c0_r, cc_s, cc_r,
    rs_s, rs_r, ag_s, ag_r, i0_s, i0_r, ix_s, ix_r, il_s, il_r, iy_s, iy_r,
):
    tok, z, fout = lax.axis_index("tok"), lax.axis_index("fin"), lax.axis_index("fout")
    y, x = tok // 2, (tok % 2) * 2 + fout // 2
    core = fout % 2
    me = core * 4 + x

    def at(y_, x_, c_, z_):
        return dict(tok=y_ * 2 + x_ // 2, fin=z_, fout=(x_ % 2) * 2 + c_)

    def row_peer(k):
        j = (me + k) % 8
        return at(y, j % 4, j // 4, z)

    partner = at(y, x, 1 - core, z)
    xpeer = [at(y, (x + d) % 4, core, z) for d in DX]
    ypeer = [None] + [at((y + d) % 4, x, core, z) for d in DY[1:]]
    zdn = at(y, x, core, (z + NZ - 1) % NZ)
    zup = at(y, x, core, (z + 1) % NZ)
    BACK = (0, 2, 1, 3)

    def rcopy(src, dst, ss, rs, dev):
        return pltpu.make_async_remote_copy(
            src_ref=src, dst_ref=dst, send_sem=ss, recv_sem=rs, device_id=dev, device_id_type=MESH
        )

    sends = []

    def start(copy):
        copy.start()
        sends.append(copy)

    loads = [
        pltpu.make_async_copy(x_hbm, xb.at[0, 0, me], w_sem.at[0]),
        pltpu.make_async_copy(ct_hbm, xb.at[0, 1, me], w_sem.at[1]),
        pltpu.make_async_copy(wg_hbm, wgu.at[:, 0:896], w_sem.at[2]),
        pltpu.make_async_copy(wu_hbm, wgu.at[:, 896:1792], w_sem.at[3]),
        pltpu.make_async_copy(wd_hbm, wd, w_sem.at[4]),
    ]
    for c in loads:
        c.start()

    bar = pltpu.get_barrier_semaphore()
    everyone = [row_peer(k) for k in range(1, 8)] + ypeer[1:] + [zdn, zup]
    for p in everyone:
        pl.semaphore_signal(bar, inc=1, device_id=p, device_id_type=MESH)
    far = [(z + 4 + 2 * r) % NZ for r in range(4)]
    for r in range(4):

        @pl.when(me == far[r])
        def _(r=r):
            for n in range(1 if r == 0 else 0, 8):
                j = (me + n) % 8
                source = at((y + 4 - DY[r]) % 4, j % 4, j // 4, z)
                pl.semaphore_signal(bar, inc=1, device_id=source, device_id_type=MESH)

    pl.semaphore_wait(bar, len(everyone) + jnp.where(me == far[0], 3, 4))

    def blk(k):
        return core * 4 + (x if k == 0 else (x + DX[k - 1]) % 4)

    def x_send(r, a, k):
        return rcopy(xb.at[r, a, me], xb.at[r, a, me], g_s.at[r, a, k], g_r.at[r, a, BACK[k]], xpeer[k - 1])

    def y_send(r, a, k):
        q = BACK[r]
        return rcopy(xb.at[0, a, blk(k)], xb.at[q, a, blk(k)], g_s.at[r, a, k], g_r.at[q, a, k], ypeer[r])

    def g_recv(r, a, k):
        dev = xpeer[k - 1] if r in (0, 3) and k > 0 else ypeer[r]
        return rcopy(xb.at[r, a, blk(k)], xb.at[r, a, blk(k)], g_s.at[r, a, k], g_r.at[r, a, k], dev)

    def c0_copy(a, k, own=True):
        b = blk(k) if own else (4 - 4 * core) + blk(k) - 4 * core
        return rcopy(xb.at[0, a, b], xb.at[0, a, b], c0_s.at[a, k], c0_r.at[a, k], partner)

    def cc_copy(r, a, own=True):
        b = pl.ds(4 * core if own else 4 - 4 * core, 4)
        return rcopy(xb.at[r, a, b], xb.at[r, a, b], cc_s.at[r, a], cc_r.at[r, a], partner)

    def own_sends():
        for a in (0, 1):
            loads[a].wait()
            for k in (1, 2, 3):
                start(x_send(0, a, k))
            start(c0_copy(a, 0))
            start(y_send(1, a, 0))
            start(y_send(2, a, 0))
        for a in (0, 1):
            start(y_send(3, a, 0))

    def row_in(a):
        for k in (1, 2, 3):
            g_recv(0, a, k).wait_recv()
            start(c0_copy(a, k))
            start(y_send(1, a, k))
            start(y_send(2, a, k))

    def third_in(a):
        g_recv(3, a, 0).wait_recv()
        for k in (1, 2, 3):
            start(x_send(3, a, k))

    nd = [4, 3, 4, 3]

    def hand_over(r):
        for a in (0, 1):
            for k in range(4):
                if r != 3 or k > 0:
                    g_recv(r, a, k).wait_recv()
            start(cc_copy(r, a))

    def partials(r):
        if r == 0:
            for k in range(4):
                c0_copy(0, k, False).wait_recv()
            loads[2].wait()
            loads[3].wait()
        else:
            cc_copy(r, 0, False).wait_recv()
        toks = xb[r, 0].reshape(128, 1024)
        both = jnp.dot(toks, wgu[...], preferred_element_type=F32)
        pt[r, :, 0] = both[:, :896].reshape(8, 16, 896)
        pt[r, :, 1] = both[:, 896:].reshape(8, 16, 896)
        if r == 0:
            for k in range(4):
                c0_copy(1, k, False).wait_recv()
            loads[4].wait()
        else:
            cc_copy(r, 1, False).wait_recv()
        cots = xb[r, 1].reshape(128, 1024)
        pt[r, :, 2] = lax.dot_general(cots, wd[...], NT, preferred_element_type=F32).reshape(8, 16, 896)
        send_sums(r, 0)
        xt[:, r * 128:r * 128 + 128] = toks.T

    def dn_copy(r, s):
        return rcopy(sdn.at[r, s], rdn.at[r, s], rs_s.at[r, 0, s], rs_r.at[r, 0, s], zdn)

    def up_copy(r, s):
        return rcopy(sup.at[r, s], rup.at[r, s], rs_s.at[r, 1, s], rs_r.at[r, 1, s], zup)

    def send_sums(r, s):
        n, m = nd[r], 7 - nd[r]
        if s < n:
            mine = pt[r, (z - n + s + NZ + 2 * r) % NZ]
            if s > 0:
                dn_copy(r, s - 1).wait_recv()
                mine = mine + rdn[r, s - 1].astype(F32)
            sdn[r, s] = mine.astype(BF)
            start(dn_copy(r, s))
        if s < m:
            mine = pt[r, (z + m - s + 2 * r) % NZ]
            if s > 0:
                up_copy(r, s - 1).wait_recv()
                mine = mine + rup[r, s - 1].astype(F32)
            sup[r, s] = mine.astype(BF)
            start(up_copy(r, s))

    def ag_copy(r, d, t, recv=False):
        t_ = t + 1 if recv else t
        c = (z + t_ + 2 * r) % NZ if d == 0 else (z - t_ + NZ + 2 * r) % NZ
        return rcopy(gb.at[r, c], gb.at[r, c], ag_s.at[r, d, t], ag_r.at[r, d, t], zdn if d == 0 else zup)

    def act(r):
        n, m = nd[r], 7 - nd[r]
        dn_copy(r, n - 1).wait_recv()
        up_copy(r, m - 1).wait_recv()
        own = (z + 2 * r) % NZ
        total = pt[r, own] + rdn[r, n - 1].astype(F32) + rup[r, m - 1].astype(F32)
        g, u, hg = total[0], total[1], total[2]
        s = jax.nn.sigmoid(g)
        silu = g * s
        gb[r, own, 2] = (silu * u).astype(BF)
        gb[r, own, 0] = (hg * u * s * (1.0 + g * (1.0 - s))).astype(BF)
        gb[r, own, 1] = (hg * silu).astype(BF)

    def spread(r, t):
        hops = (7 - nd[r], nd[r])
        for d in (0, 1):
            if 0 < t <= hops[d]:
                ag_copy(r, d, t - 1, True).wait_recv()
            if t < hops[d]:
                start(ag_copy(r, d, t))

    def stage(r, s):
        if s < 4:
            send_sums(r, s)
        else:
            if s == 4:
                act(r)
            spread(r, s - 4)

    def p0_copy(r, i):
        return rcopy(igs.at[r, 4 - 4 * core + i], igr.at[r, i], i0_s.at[r, i], i0_r.at[r, i], partner)

    def px_copy(r, n):
        m = BACK[n + 1] - 1
        return rcopy(ips.at[r, (x + DX[n]) % 4], ipr.at[r, m], ix_s.at[r, n], ix_r.at[r, m], xpeer[n])

    def px_recv(r, n):
        return rcopy(ips.at[r, 0], ipr.at[r, n], ix_s.at[r, n], ix_r.at[r, n], xpeer[n])

    def late_copy(r):
        owner = at((y + DY[r]) % 4, far[r] % 4, far[r] // 4, z)
        n = (me - far[r] + 8) % 8
        return rcopy(ils.at[r], ilr.at[n], il_s.at[r], il_r.at[n], owner)

    def late_recv(n):
        return rcopy(ils.at[0], ilr.at[n], il_s.at[0], il_r.at[n], partner)

    def input_rows(chunks):
        both = jnp.concatenate(
            [jnp.concatenate([gb[r, c, 0], gb[r, c, 1]], axis=1) for r, c in chunks], axis=0
        )
        return lax.dot_general(both, wgu[...], NT, preferred_element_type=F32).astype(BF)

    def input_early(r):
        chunks = [(r, (z + n + NZ + 2 * r) % NZ) for n in range(-3, 4)]
        part = input_rows(chunks)
        for n, (_, c) in enumerate(chunks):
            igs[r, c] = part[16 * n:16 * n + 16]
        for i in range(4):

            @pl.when(4 - 4 * core + i != far[r])
            def _(i=i):
                p0_copy(r, i).start()

    def pair_early(r):
        for n in range(4):
            i = (x + ((0,) + DX)[n]) % 4

            @pl.when(4 * core + i != far[r])
            def _(i=i, n=n):
                p0_copy(r, i).wait_recv()
                own = igs[r, 4 * core + i]
                ips[r, i] = (own.astype(F32) + igr[r, i].astype(F32)).astype(BF)
                if n > 0:
                    px_copy(r, n - 1).start()

    def input_late():
        part = input_rows([(r, far[r]) for r in range(4)])
        for r in range(4):
            ils[r] = part[16 * r:16 * r + 16]
            if r > 0:
                start(late_copy(r))

        @pl.when(me != far[0])
        def _():
            late_copy(0).start()

    def row_total(r):
        v = ips[r, x].astype(F32)
        for n in range(3):
            px_recv(r, n).wait_recv()
            v = v + ipr[r, n].astype(F32)
        return v

    def row_sum(r):
        @pl.when(me != far[r])
        def _():
            iys[r] = row_total(r).astype(BF)
            iy_copy(r).start()

    def early_end(r):
        for i in range(4):

            @pl.when(4 - 4 * core + i != far[r])
            def _(i=i):
                p0_copy(r, i).wait_send()

        for n in range(3):

            @pl.when(4 * core + (x + DX[n]) % 4 != far[r])
            def _(n=n):
                px_copy(r, n).wait_send()

        @pl.when(me != far[r])
        def _():
            if r == 0:
                late_copy(0).wait_send()
            else:
                iy_copy(r).wait_send()

    def add_dw(lhs, rhs, out):
        width = rhs.shape[1]
        for c in range(0, width, 256):
            e = min(c + 256, width)
            out[:, c:e] = jnp.dot(lhs[...], rhs[:, c:e], preferred_element_type=F32).astype(BF)

    def turn_hidden(r):
        ht[:, r * 128:r * 128 + 128] = gb[r, :, 2].reshape(128, 896).T

    def weights_part(n):
        if n < 2:
            add_dw(xt, gb[:, :, n].reshape(512, 896), (dwg_out, dwu_out)[n])
        else:
            add_dw(ht, xb[:, 1].reshape(512, 1024), dwd_out)

    def iy_copy(r):
        return rcopy(iys.at[r], iyr.at[r], iy_s.at[r], iy_r.at[r], ypeer[r])

    def finish():
        igacc[...] = jnp.zeros_like(igacc)
        for r in (3, 2, 1, 0):

            @pl.when(me != far[r])
            def _(r=r):
                if r == 0:
                    igacc[...] += row_total(0)
                else:
                    iy_copy(r).wait_recv()
                    igacc[...] += iyr[r].astype(F32)

        for r in range(4):

            @pl.when(me == far[r])
            def _(r=r):
                v = igacc[...]
                if r == 0:
                    v = v + ils[0].astype(F32)
                for n in range(1 if r == 0 else 0, 8):
                    late_recv(n).wait_recv()
                    v = v + ilr[n].astype(F32)
                igacc[...] = v

        ig_out[...] = igacc[...].astype(BF)
        for r in range(4):
            early_end(r)

    steps = []

    def then(fn, *given):
        steps.append((fn, given))

    then(own_sends)
    then(row_in, 0)
    then(row_in, 1)
    then(third_in, 0)
    then(third_in, 1)
    then(partials, 0)
    then(hand_over, 1)
    then(hand_over, 2)
    then(partials, 1)
    then(partials, 2)
    then(stage, 0, 1)
    then(hand_over, 3)
    then(partials, 3)
    then(stage, 1, 1)
    then(stage, 2, 1)
    then(stage, 0, 2)
    done, last = [2, 1, 1, 0], [2, 0]
    while min(done) < 6:
        free = [q for q in (3, 2, 1, 0) if q not in last[-2:] and done[q] < 6]
        r = min(free or (3, 2, 1, 0), key=lambda q: done[q])
        done[r] += 1
        last.append(r)
        then(stage, r, done[r])
    then(stage, 3, 7)
    then(input_early, 3)
    then(stage, 2, 7)
    then(input_early, 2)
    then(pair_early, 3)
    then(stage, 1, 7)
    then(input_early, 1)
    then(pair_early, 2)
    then(stage, 0, 7)
    then(input_early, 0)
    then(pair_early, 1)
    for r in (3, 2, 1, 0):
        then(stage, r, 8)
    then(input_late)
    then(pair_early, 0)
    for r in range(4):
        then(turn_hidden, r)
    then(row_sum, 3)
    then(row_sum, 2)
    then(row_sum, 1)
    for n in range(3):
        then(weights_part, n)
    then(finish)
    for fn, given in steps:
        fn(*given)
    for c in sends:
        c.wait_send()


def writer(*refs):
    sem = refs[8]
    copies = [pltpu.make_async_copy(refs[i], refs[4 + i], sem.at[i]) for i in range(4)]
    for c in copies:
        c.start()
    for c in copies:
        c.wait()


def local(tokens_in, cotangent, gate_weight, up_weight, down_weight):
    vm = pltpu.VMEM
    dma = pltpu.SemaphoreType.DMA
    outs = pl.pallas_call(
        kernel,
        out_shape=(
            pltpu.VMEM((16, 1024), BF),
            pltpu.VMEM((1024, 896), BF),
            pltpu.VMEM((1024, 896), BF),
            pltpu.VMEM((896, 1024), BF),
        ),
        in_specs=[pl.BlockSpec(memory_space=pl.ANY)] * 5,
        out_specs=[pl.BlockSpec(memory_space=pltpu.VMEM)] * 4,
        scratch_shapes=[
            vm((4, 2, 8, 16, 1024), BF),
            vm((1024, 512), BF),
            vm((896, 512), BF),
            vm((1024, 1792), BF),
            vm((896, 1024), BF),
            vm((4, 8, 3, 16, 896), F32),
            vm((4, 4, 3, 16, 896), BF),
            vm((4, 4, 3, 16, 896), BF),
            vm((4, 4, 3, 16, 896), BF),
            vm((4, 4, 3, 16, 896), BF),
            vm((4, 8, 3, 16, 896), BF),
            vm((4, 8, 16, 1024), BF),
            vm((4, 4, 16, 1024), BF),
            vm((4, 4, 16, 1024), BF),
            vm((4, 3, 16, 1024), BF),
            vm((4, 16, 1024), BF),
            vm((8, 16, 1024), BF),
            vm((4, 16, 1024), BF),
            vm((4, 16, 1024), BF),
            vm((16, 1024), F32),
            dma((5,)),
            dma((4, 2, 4)), dma((4, 2, 4)),
            dma((2, 4)), dma((2, 4)),
            dma((4, 2)), dma((4, 2)),
            dma((4, 2, 4)), dma((4, 2, 4)),
            dma((4, 2, 4)), dma((4, 2, 4)),
            dma((4, 4)), dma((4, 4)),
            dma((4, 3)), dma((4, 3)),
            dma((4,)), dma((8,)),
            dma((4,)), dma((4,)),
        ],
        compiler_params=pltpu.CompilerParams(
            collective_id=0, has_side_effects=True, vmem_limit_bytes=48 * 2**20
        ),
        cost_estimate=pl.CostEstimate(flops=7_516_000_000, bytes_accessed=11_000_000, transcendentals=0),
    )(tokens_in, cotangent, gate_weight, up_weight, down_weight)
    outs = [pltpu.with_memory_space_constraint(a, pltpu.MemorySpace.VMEM) for a in outs]
    return pl.pallas_call(
        writer,
        out_shape=(
            jax.ShapeDtypeStruct((16, 1024), BF),
            jax.ShapeDtypeStruct((1024, 896), BF),
            jax.ShapeDtypeStruct((1024, 896), BF),
            jax.ShapeDtypeStruct((896, 1024), BF),
        ),
        in_specs=[pl.BlockSpec(memory_space=pltpu.VMEM)] * 4,
        out_specs=[pl.BlockSpec(memory_space=pl.ANY)] * 4,
        scratch_shapes=[pltpu.SemaphoreType.DMA((4,))],
        compiler_params=pltpu.CompilerParams(vmem_limit_bytes=2**20),
        cost_estimate=pl.CostEstimate(flops=0, bytes_accessed=11_000_000, transcendentals=0),
    )(*outs)


def solution(mesh):
    in_specs = (
        P(("tok", "fout"), "fin"),
        P(("tok", "fout"), "fin"),
        P("fin", ("tok", "fout")),
        P("fin", ("tok", "fout")),
        P(("tok", "fout"), "fin"),
    )
    out_specs = (
        P(("tok", "fout"), "fin"),
        P("fin", ("tok", "fout")),
        P("fin", ("tok", "fout")),
        P(("tok", "fout"), "fin"),
    )
    return jax.shard_map(local, mesh=mesh, in_specs=in_specs, out_specs=out_specs, check_vma=False)
```

```python
import functools

import jax
import jax.numpy as jnp
from jax import lax
from jax.experimental import pallas as pl
from jax.experimental.pallas import tpu as pltpu
from jax.sharding import PartitionSpec as P

MESH = pl.DeviceIdType.MESH
BF = jnp.bfloat16
F32 = jnp.float32
NT = (((1,), (1,)), ((), ()))
DY = (0, 1, 3, 2)
DX = (1, 3, 2)
NZ = 8
NR = 4


def kernel(
    x_hbm, ct_hbm, wg_hbm, wu_hbm, wd_hbm,
    ig_out, dwg_out, dwu_out, dwd_out,
    xb, xt, ht, wgu, wd, pt, sdn, sup, rdn, rup, gb, igs, igr, ips, ipr, ils, ilr, iys, iyr, igacc,
    w_sem, g_s, g_r, c_s, c_r, f_s, f_r,
    rs_s, rs_r, ag_s, ag_r, i0_s, i0_r, ix_s, ix_r, il_s, il_r, iy_s, iy_r,
):
    tok, z, fout = lax.axis_index("tok"), lax.axis_index("fin"), lax.axis_index("fout")
    y, x = tok // 2, (tok % 2) * 2 + fout // 2
    core = fout % 2
    me = core * 4 + x

    def at(y_, x_, c_, z_):
        return dict(tok=y_ * 2 + x_ // 2, fin=z_, fout=(x_ % 2) * 2 + c_)

    def row_peer(k):
        j = (me + k) % 8
        return at(y, j % 4, j // 4, z)

    partner = at(y, x, 1 - core, z)
    xpeer = [at(y, (x + d) % 4, core, z) for d in DX]
    ypeer = [None] + [at((y + d) % 4, x, core, z) for d in DY[1:]]
    zdn = at(y, x, core, (z + NZ - 1) % NZ)
    zup = at(y, x, core, (z + 1) % NZ)
    BACK = (0, 2, 1, 3)

    def rcopy(src, dst, ss, rs, dev):
        return pltpu.make_async_remote_copy(
            src_ref=src, dst_ref=dst, send_sem=ss, recv_sem=rs, device_id=dev, device_id_type=MESH
        )

    sends = []

    def start(copy):
        copy.start()
        sends.append(copy)

    loads = [
        pltpu.make_async_copy(x_hbm, xb.at[0, 0, me], w_sem.at[0]),
        pltpu.make_async_copy(ct_hbm, xb.at[0, 1, me], w_sem.at[1]),
        pltpu.make_async_copy(wg_hbm, wgu.at[:, 0:896], w_sem.at[2]),
        pltpu.make_async_copy(wu_hbm, wgu.at[:, 896:1792], w_sem.at[3]),
        pltpu.make_async_copy(wd_hbm, wd, w_sem.at[4]),
    ]
    for c in loads:
        c.start()

    bar = pltpu.get_barrier_semaphore()
    everyone = [row_peer(k) for k in range(1, 8)] + ypeer[1:] + [zdn, zup]
    for p in everyone:
        pl.semaphore_signal(bar, inc=1, device_id=p, device_id_type=MESH)
    far = [(z + 4 + 2 * r) % NZ for r in range(4)]
    for r in range(4):

        @pl.when(me == far[r])
        def _(r=r):
            for n in range(1 if r == 0 else 0, 8):
                j = (me + n) % 8
                source = at((y + 4 - DY[r]) % 4, j % 4, j // 4, z)
                pl.semaphore_signal(bar, inc=1, device_id=source, device_id_type=MESH)

    pl.semaphore_wait(bar, len(everyone) + jnp.where(me == far[0], 3, 4))

    def blk(k):
        return core * 4 + (x if k == 0 else (x + DX[k - 1]) % 4)

    def x_send(r, a, k):
        return rcopy(xb.at[r, a, me], xb.at[r, a, me], g_s.at[r, a, k], g_r.at[r, a, BACK[k]], xpeer[k - 1])

    def y_send(r, a, k):
        q = BACK[r]
        return rcopy(xb.at[0, a, blk(k)], xb.at[q, a, blk(k)], g_s.at[r, a, k], g_r.at[q, a, k], ypeer[r])

    def g_recv(r, a, k):
        dev = xpeer[k - 1] if r in (0, 3) and k > 0 else ypeer[r]
        return rcopy(xb.at[r, a, blk(k)], xb.at[r, a, blk(k)], g_s.at[r, a, k], g_r.at[r, a, k], dev)

    def c_copy(r, a, k, own=True):
        b = blk(k) if own else (4 - 4 * core) + blk(k) - 4 * core
        return rcopy(xb.at[r, a, b], xb.at[r, a, b], c_s.at[r, a, k], c_r.at[r, a, k], partner)

    def own_sends():
        for a in (0, 1):
            loads[a].wait()
            for k in (1, 2, 3):
                start(x_send(0, a, k))
            start(c_copy(0, a, 0))
            start(y_send(1, a, 0))
            start(y_send(2, a, 0))
        for a in (0, 1):
            start(y_send(3, a, 0))

    def row_in(a):
        for k in (1, 2, 3):
            g_recv(0, a, k).wait_recv()
            start(c_copy(0, a, k))
            start(y_send(1, a, k))
            start(y_send(2, a, k))

    def third_in(a):
        g_recv(3, a, 0).wait_recv()
        for k in (1, 2, 3):
            start(x_send(3, a, k))

    nd = [4, 3, 4, 3]

    def hand_over(*rounds):
        for a in (0, 1):
            for k in range(4):
                for r in rounds:
                    if r != 3 or k > 0:
                        g_recv(r, a, k).wait_recv()
                    start(c_copy(r, a, k))

    def first_copy(d, part):
        b = pl.ds(0, 2) if part == 0 else pl.ds(2, 1)
        src, dst = (sdn, rdn) if d == 0 else (sup, rup)
        return rcopy(
            src.at[0, 0, b], dst.at[0, 0, b], f_s.at[d, part], f_r.at[d, part], zdn if d == 0 else zup
        )

    def first_sums(part):
        b = slice(0, 2) if part == 0 else slice(2, 3)
        sdn[0, 0, b] = pt[0, (z - nd[0] + NZ) % NZ, b].astype(BF)
        start(first_copy(0, part))
        sup[0, 0, b] = pt[0, (z + 7 - nd[0]) % NZ, b].astype(BF)
        start(first_copy(1, part))

    def partials(r):
        for k in range(4):
            c_copy(r, 0, k, False).wait_recv()
        if r == 0:
            loads[2].wait()
            loads[3].wait()
        toks = xb[r, 0].reshape(128, 1024)
        both = jnp.dot(toks, wgu[...], preferred_element_type=F32)
        pt[r, :, 0] = both[:, :896].reshape(8, 16, 896)
        pt[r, :, 1] = both[:, 896:].reshape(8, 16, 896)
        if r == 0:
            first_sums(0)
            loads[4].wait()
        for k in range(4):
            c_copy(r, 1, k, False).wait_recv()
        cots = xb[r, 1].reshape(128, 1024)
        pt[r, :, 2] = lax.dot_general(cots, wd[...], NT, preferred_element_type=F32).reshape(8, 16, 896)
        if r == 0:
            first_sums(1)
        else:
            send_sums(r, 0)
        xt[:, r * 128:r * 128 + 128] = toks.T

    def dn_copy(r, s):
        return rcopy(sdn.at[r, s], rdn.at[r, s], rs_s.at[r, 0, s], rs_r.at[r, 0, s], zdn)

    def up_copy(r, s):
        return rcopy(sup.at[r, s], rup.at[r, s], rs_s.at[r, 1, s], rs_r.at[r, 1, s], zup)

    def arrived(r, d, s):
        if r == 0 and s == 0:
            for part in (0, 1):
                first_copy(d, part).wait_recv()
        else:
            (dn_copy, up_copy)[d](r, s).wait_recv()

    def send_sums(r, s):
        n, m = nd[r], 7 - nd[r]
        if s < n:
            mine = pt[r, (z - n + s + NZ + 2 * r) % NZ]
            if s > 0:
                arrived(r, 0, s - 1)
                mine = mine + rdn[r, s - 1].astype(F32)
            sdn[r, s] = mine.astype(BF)
            start(dn_copy(r, s))
        if s < m:
            mine = pt[r, (z + m - s + 2 * r) % NZ]
            if s > 0:
                arrived(r, 1, s - 1)
                mine = mine + rup[r, s - 1].astype(F32)
            sup[r, s] = mine.astype(BF)
            start(up_copy(r, s))

    def ag_copy(r, d, t, recv=False):
        t_ = t + 1 if recv else t
        c = (z + t_ + 2 * r) % NZ if d == 0 else (z - t_ + NZ + 2 * r) % NZ
        return rcopy(gb.at[r, c], gb.at[r, c], ag_s.at[r, d, t], ag_r.at[r, d, t], zdn if d == 0 else zup)

    def act(r):
        n, m = nd[r], 7 - nd[r]
        dn_copy(r, n - 1).wait_recv()
        up_copy(r, m - 1).wait_recv()
        own = (z + 2 * r) % NZ
        total = pt[r, own] + rdn[r, n - 1].astype(F32) + rup[r, m - 1].astype(F32)
        g, u, hg = total[0], total[1], total[2]
        s = jax.nn.sigmoid(g)
        silu = g * s
        gb[r, own, 2] = (silu * u).astype(BF)
        gb[r, own, 0] = (hg * u * s * (1.0 + g * (1.0 - s))).astype(BF)
        gb[r, own, 1] = (hg * silu).astype(BF)

    def spread(r, t):
        hops = (7 - nd[r], nd[r])
        for d in (0, 1):
            if 0 < t <= hops[d]:
                ag_copy(r, d, t - 1, True).wait_recv()
            if t < hops[d]:
                start(ag_copy(r, d, t))

    def stage(r, s):
        if s < 4:
            send_sums(r, s)
        else:
            if s == 4:
                act(r)
            spread(r, s - 4)

    def p0_copy(r, i):
        return rcopy(igs.at[r, 4 - 4 * core + i], igr.at[r, i], i0_s.at[r, i], i0_r.at[r, i], partner)

    def px_copy(r, n):
        m = BACK[n + 1] - 1
        return rcopy(ips.at[r, (x + DX[n]) % 4], ipr.at[r, m], ix_s.at[r, n], ix_r.at[r, m], xpeer[n])

    def px_recv(r, n):
        return rcopy(ips.at[r, 0], ipr.at[r, n], ix_s.at[r, n], ix_r.at[r, n], xpeer[n])

    def late_copy(r):
        owner = at((y + DY[r]) % 4, far[r] % 4, far[r] // 4, z)
        n = (me - far[r] + 8) % 8
        return rcopy(ils.at[r], ilr.at[n], il_s.at[r], il_r.at[n], owner)

    def late_recv(n):
        return rcopy(ils.at[0], ilr.at[n], il_s.at[0], il_r.at[n], partner)

    def input_rows(chunks):
        both = jnp.concatenate(
            [jnp.concatenate([gb[r, c, 0], gb[r, c, 1]], axis=1) for r, c in chunks], axis=0
        )
        return lax.dot_general(both, wgu[...], NT, preferred_element_type=F32).astype(BF)

    def input_early(r):
        chunks = [(r, (z + n + NZ + 2 * r) % NZ) for n in range(-3, 4)]
        part = input_rows(chunks)
        for n, (_, c) in enumerate(chunks):
            igs[r, c] = part[16 * n:16 * n + 16]
        for i in range(4):

            @pl.when(4 - 4 * core + i != far[r])
            def _(i=i):
                p0_copy(r, i).start()

    def pair_early(r):
        for n in range(4):
            i = (x + ((0,) + DX)[n]) % 4

            @pl.when(4 * core + i != far[r])
            def _(i=i, n=n):
                p0_copy(r, i).wait_recv()
                own = igs[r, 4 * core + i]
                ips[r, i] = (own.astype(F32) + igr[r, i].astype(F32)).astype(BF)
                if n > 0:
                    px_copy(r, n - 1).start()

    def input_late(*rounds):
        part = input_rows([(r, far[r]) for r in rounds])
        for n, r in enumerate(rounds):
            ils[r] = part[16 * n:16 * n + 16]
            if r > 0:
                start(late_copy(r))
            else:

                @pl.when(me != far[0])
                def _():
                    late_copy(0).start()

    def row_total(r):
        v = ips[r, x].astype(F32)
        for n in range(3):
            px_recv(r, n).wait_recv()
            v = v + ipr[r, n].astype(F32)
        return v

    def row_sum(r):
        @pl.when(me != far[r])
        def _():
            iys[r] = row_total(r).astype(BF)
            iy_copy(r).start()

    def early_end(r):
        for i in range(4):

            @pl.when(4 - 4 * core + i != far[r])
            def _(i=i):
                p0_copy(r, i).wait_send()

        for n in range(3):

            @pl.when(4 * core + (x + DX[n]) % 4 != far[r])
            def _(n=n):
                px_copy(r, n).wait_send()

        @pl.when(me != far[r])
        def _():
            if r == 0:
                late_copy(0).wait_send()
            else:
                iy_copy(r).wait_send()

    def add_dw(lhs, rhs, out):
        width = rhs.shape[1]
        for c in range(0, width, 256):
            e = min(c + 256, width)
            out[:, c:e] = jnp.dot(lhs[...], rhs[:, c:e], preferred_element_type=F32).astype(BF)

    def turn_hidden(r):
        ht[:, r * 128:r * 128 + 128] = gb[r, :, 2].reshape(128, 896).T

    def weights_part(n):
        if n < 2:
            add_dw(xt, gb[:, :, n].reshape(512, 896), (dwg_out, dwu_out)[n])
        else:
            add_dw(ht, xb[:, 1].reshape(512, 1024), dwd_out)

    def iy_copy(r):
        return rcopy(iys.at[r], iyr.at[r], iy_s.at[r], iy_r.at[r], ypeer[r])

    def finish():
        igacc[...] = jnp.zeros_like(igacc)
        for r in (3, 2, 1, 0):

            @pl.when(me != far[r])
            def _(r=r):
                if r == 0:
                    igacc[...] += row_total(0)
                else:
                    iy_copy(r).wait_recv()
                    igacc[...] += iyr[r].astype(F32)

        for r in range(4):

            @pl.when(me == far[r])
            def _(r=r):
                v = igacc[...]
                if r == 0:
                    v = v + ils[0].astype(F32)
                for n in range(1 if r == 0 else 0, 8):
                    late_recv(n).wait_recv()
                    v = v + ilr[n].astype(F32)
                igacc[...] = v

        ig_out[...] = igacc[...].astype(BF)
        for r in range(4):
            early_end(r)

    steps = []

    def then(fn, *given):
        steps.append((fn, given))

    then(own_sends)
    then(row_in, 0)
    then(row_in, 1)
    then(partials, 0)
    then(third_in, 0)
    then(third_in, 1)
    then(hand_over, 1)
    then(partials, 1)
    then(hand_over, 2)
    then(stage, 0, 1)
    then(partials, 2)
    then(hand_over, 3)
    then(partials, 3)
    then(stage, 1, 1)
    then(stage, 0, 2)
    then(stage, 2, 1)
    done, last = [2, 1, 1, 0], [0, 2]
    while min(done) < 6:
        free = [q for q in (3, 2, 1, 0) if q not in last[-2:] and done[q] < 6]
        r = min(free or (3, 2, 1, 0), key=lambda q: done[q])
        done[r] += 1
        last.append(r)
        then(stage, r, done[r])
    then(stage, 3, 7)
    then(input_early, 3)
    then(stage, 2, 7)
    then(input_early, 2)
    then(pair_early, 3)
    then(stage, 1, 7)
    then(input_early, 1)
    then(pair_early, 2)
    then(stage, 0, 7)
    then(input_early, 0)
    then(pair_early, 1)
    then(stage, 3, 8)
    then(stage, 2, 8)
    then(input_late, 3, 2)
    then(pair_early, 0)
    then(stage, 1, 8)
    then(stage, 0, 8)
    then(input_late, 1, 0)
    for r in range(4):
        then(turn_hidden, r)
    then(row_sum, 3)
    then(row_sum, 2)
    then(row_sum, 1)
    for n in range(3):
        then(weights_part, n)
    then(finish)
    for fn, given in steps:
        fn(*given)
    for c in sends:
        c.wait_send()


def writer(*refs):
    sem = refs[8]
    copies = [pltpu.make_async_copy(refs[i], refs[4 + i], sem.at[i]) for i in range(4)]
    for c in copies:
        c.start()
    for c in copies:
        c.wait()


def local(tokens_in, cotangent, gate_weight, up_weight, down_weight):
    vm = pltpu.VMEM
    dma = pltpu.SemaphoreType.DMA
    outs = pl.pallas_call(
        kernel,
        out_shape=(
            pltpu.VMEM((16, 1024), BF),
            pltpu.VMEM((1024, 896), BF),
            pltpu.VMEM((1024, 896), BF),
            pltpu.VMEM((896, 1024), BF),
        ),
        in_specs=[pl.BlockSpec(memory_space=pl.ANY)] * 5,
        out_specs=[pl.BlockSpec(memory_space=pltpu.VMEM)] * 4,
        scratch_shapes=[
            vm((4, 2, 8, 16, 1024), BF),
            vm((1024, 512), BF),
            vm((896, 512), BF),
            vm((1024, 1792), BF),
            vm((896, 1024), BF),
            vm((4, 8, 3, 16, 896), F32),
            vm((4, 4, 3, 16, 896), BF),
            vm((4, 4, 3, 16, 896), BF),
            vm((4, 4, 3, 16, 896), BF),
            vm((4, 4, 3, 16, 896), BF),
            vm((4, 8, 3, 16, 896), BF),
            vm((4, 8, 16, 1024), BF),
            vm((4, 4, 16, 1024), BF),
            vm((4, 4, 16, 1024), BF),
            vm((4, 3, 16, 1024), BF),
            vm((4, 16, 1024), BF),
            vm((8, 16, 1024), BF),
            vm((4, 16, 1024), BF),
            vm((4, 16, 1024), BF),
            vm((16, 1024), F32),
            dma((5,)),
            dma((4, 2, 4)), dma((4, 2, 4)),
            dma((4, 2, 4)), dma((4, 2, 4)),
            dma((2, 2)), dma((2, 2)),
            dma((4, 2, 4)), dma((4, 2, 4)),
            dma((4, 2, 4)), dma((4, 2, 4)),
            dma((4, 4)), dma((4, 4)),
            dma((4, 3)), dma((4, 3)),
            dma((4,)), dma((8,)),
            dma((4,)), dma((4,)),
        ],
        compiler_params=pltpu.CompilerParams(
            collective_id=0, has_side_effects=True, vmem_limit_bytes=48 * 2**20
        ),
        cost_estimate=pl.CostEstimate(flops=7_516_000_000, bytes_accessed=11_000_000, transcendentals=0),
    )(tokens_in, cotangent, gate_weight, up_weight, down_weight)
    outs = [pltpu.with_memory_space_constraint(a, pltpu.MemorySpace.VMEM) for a in outs]
    return pl.pallas_call(
        writer,
        out_shape=(
            jax.ShapeDtypeStruct((16, 1024), BF),
            jax.ShapeDtypeStruct((1024, 896), BF),
            jax.ShapeDtypeStruct((1024, 896), BF),
            jax.ShapeDtypeStruct((896, 1024), BF),
        ),
        in_specs=[pl.BlockSpec(memory_space=pltpu.VMEM)] * 4,
        out_specs=[pl.BlockSpec(memory_space=pl.ANY)] * 4,
        scratch_shapes=[pltpu.SemaphoreType.DMA((4,))],
        compiler_params=pltpu.CompilerParams(vmem_limit_bytes=2**20),
        cost_estimate=pl.CostEstimate(flops=0, bytes_accessed=11_000_000, transcendentals=0),
    )(*outs)


def solution(mesh):
    in_specs = (
        P(("tok", "fout"), "fin"),
        P(("tok", "fout"), "fin"),
        P("fin", ("tok", "fout")),
        P("fin", ("tok", "fout")),
        P(("tok", "fout"), "fin"),
    )
    out_specs = (
        P(("tok", "fout"), "fin"),
        P("fin", ("tok", "fout")),
        P("fin", ("tok", "fout")),
        P(("tok", "fout"), "fin"),
    )
    return jax.shard_map(local, mesh=mesh, in_specs=in_specs, out_specs=out_specs, check_vma=False)
```

```python
import functools

import jax
import jax.numpy as jnp
from jax import lax
from jax.experimental import pallas as pl
from jax.experimental.pallas import tpu as pltpu
from jax.sharding import PartitionSpec as P

MESH = pl.DeviceIdType.MESH
BF = jnp.bfloat16
F32 = jnp.float32
NT = (((1,), (1,)), ((), ()))
DY = (0, 1, 3, 2)
DX = (1, 3, 2)
NZ = 8
NR = 4


def kernel(
    x_hbm, ct_hbm, wg_hbm, wu_hbm, wd_hbm,
    ig_out, dwg_out, dwu_out, dwd_out,
    xb, xt, ht, wgu, wd, pt, sdn, sup, rdn, rup, gb, igs, igr, ips, ipr, ils, ilr, iys, iyr, igacc,
    w_sem, g_s, g_r, c_s, c_r, f_s, f_r,
    rs_s, rs_r, ag_s, ag_r, i0_s, i0_r, ix_s, ix_r, il_s, il_r, iy_s, iy_r,
):
    tok, z, fout = lax.axis_index("tok"), lax.axis_index("fin"), lax.axis_index("fout")
    y, x = tok // 2, (tok % 2) * 2 + fout // 2
    core = fout % 2
    me = core * 4 + x

    def at(y_, x_, c_, z_):
        return dict(tok=y_ * 2 + x_ // 2, fin=z_, fout=(x_ % 2) * 2 + c_)

    def row_peer(k):
        j = (me + k) % 8
        return at(y, j % 4, j // 4, z)

    partner = at(y, x, 1 - core, z)
    xpeer = [at(y, (x + d) % 4, core, z) for d in DX]
    ypeer = [None] + [at((y + d) % 4, x, core, z) for d in DY[1:]]
    zdn = at(y, x, core, (z + NZ - 1) % NZ)
    zup = at(y, x, core, (z + 1) % NZ)
    BACK = (0, 2, 1, 3)

    def rcopy(src, dst, ss, rs, dev):
        return pltpu.make_async_remote_copy(
            src_ref=src, dst_ref=dst, send_sem=ss, recv_sem=rs, device_id=dev, device_id_type=MESH
        )

    sends = []

    def start(copy):
        copy.start()
        sends.append(copy)

    loads = [
        pltpu.make_async_copy(x_hbm, xb.at[0, 0, me], w_sem.at[0]),
        pltpu.make_async_copy(ct_hbm, xb.at[0, 1, me], w_sem.at[1]),
        pltpu.make_async_copy(wg_hbm, wgu.at[:, 0:896], w_sem.at[2]),
        pltpu.make_async_copy(wu_hbm, wgu.at[:, 896:1792], w_sem.at[3]),
        pltpu.make_async_copy(wd_hbm, wd, w_sem.at[4]),
    ]
    for c in loads:
        c.start()

    bar = pltpu.get_barrier_semaphore()
    everyone = [row_peer(k) for k in range(1, 8)] + ypeer[1:] + [zdn, zup]
    for p in everyone:
        pl.semaphore_signal(bar, inc=1, device_id=p, device_id_type=MESH)
    far = [(z + 4 + 2 * r) % NZ for r in range(4)]
    for r in range(4):

        @pl.when(me == far[r])
        def _(r=r):
            for n in range(1 if r == 0 else 0, 8):
                j = (me + n) % 8
                source = at((y + 4 - DY[r]) % 4, j % 4, j // 4, z)
                pl.semaphore_signal(bar, inc=1, device_id=source, device_id_type=MESH)

    pl.semaphore_wait(bar, len(everyone) + jnp.where(me == far[0], 3, 4))

    def blk(k):
        return core * 4 + (x if k == 0 else (x + DX[k - 1]) % 4)

    def x_send(r, a, k):
        return rcopy(xb.at[r, a, me], xb.at[r, a, me], g_s.at[r, a, k], g_r.at[r, a, BACK[k]], xpeer[k - 1])

    def y_send(r, a, k):
        q = BACK[r]
        return rcopy(xb.at[0, a, blk(k)], xb.at[q, a, blk(k)], g_s.at[r, a, k], g_r.at[q, a, k], ypeer[r])

    def g_recv(r, a, k):
        dev = xpeer[k - 1] if r in (0, 3) and k > 0 else ypeer[r]
        return rcopy(xb.at[r, a, blk(k)], xb.at[r, a, blk(k)], g_s.at[r, a, k], g_r.at[r, a, k], dev)

    def c_copy(r, a, k, own=True):
        b = blk(k) if own else (4 - 4 * core) + blk(k) - 4 * core
        return rcopy(xb.at[r, a, b], xb.at[r, a, b], c_s.at[r, a, k], c_r.at[r, a, k], partner)

    def own_sends():
        for a in (0, 1):
            loads[a].wait()
            for k in (1, 2, 3):
                start(x_send(0, a, k))
            start(c_copy(0, a, 0))
            start(y_send(1, a, 0))
            start(y_send(2, a, 0))
        for a in (0, 1):
            start(y_send(3, a, 0))

    def row_in(a):
        for k in (1, 2, 3):
            g_recv(0, a, k).wait_recv()
            start(c_copy(0, a, k))
            start(y_send(1, a, k))
            start(y_send(2, a, k))

    def third_in(a):
        g_recv(3, a, 0).wait_recv()
        for k in (1, 2, 3):
            start(x_send(3, a, k))

    nd = [4, 3, 4, 3]

    def hand_over(*rounds):
        for a in (0, 1):
            for k in range(4):
                for r in rounds:
                    if r != 3 or k > 0:
                        g_recv(r, a, k).wait_recv()
                    start(c_copy(r, a, k))

    def first_copy(d, part):
        b = pl.ds(0, 2) if part == 0 else pl.ds(2, 1)
        src, dst = (sdn, rdn) if d == 0 else (sup, rup)
        return rcopy(
            src.at[0, 0, b], dst.at[0, 0, b], f_s.at[d, part], f_r.at[d, part], zdn if d == 0 else zup
        )

    def first_sums(part):
        b = slice(0, 2) if part == 0 else slice(2, 3)
        sdn[0, 0, b] = pt[0, (z - nd[0] + NZ) % NZ, b].astype(BF)
        start(first_copy(0, part))
        sup[0, 0, b] = pt[0, (z + 7 - nd[0]) % NZ, b].astype(BF)
        start(first_copy(1, part))

    def partials(r):
        for k in range(4):
            c_copy(r, 0, k, False).wait_recv()
        if r == 0:
            loads[2].wait()
            loads[3].wait()
        toks = xb[r, 0].reshape(128, 1024)
        both = jnp.dot(toks, wgu[...], preferred_element_type=F32)
        pt[r, :, 0] = both[:, :896].reshape(8, 16, 896)
        pt[r, :, 1] = both[:, 896:].reshape(8, 16, 896)
        if r == 0:
            first_sums(0)
            loads[4].wait()
        for k in range(4):
            c_copy(r, 1, k, False).wait_recv()
        cots = xb[r, 1].reshape(128, 1024)
        pt[r, :, 2] = lax.dot_general(cots, wd[...], NT, preferred_element_type=F32).reshape(8, 16, 896)
        if r == 0:
            first_sums(1)
        else:
            send_sums(r, 0)
        xt[:, r * 128:r * 128 + 128] = toks.T

    def dn_copy(r, s):
        return rcopy(sdn.at[r, s], rdn.at[r, s], rs_s.at[r, 0, s], rs_r.at[r, 0, s], zdn)

    def up_copy(r, s):
        return rcopy(sup.at[r, s], rup.at[r, s], rs_s.at[r, 1, s], rs_r.at[r, 1, s], zup)

    def arrived(r, d, s):
        if r == 0 and s == 0:
            for part in (0, 1):
                first_copy(d, part).wait_recv()
        else:
            (dn_copy, up_copy)[d](r, s).wait_recv()

    def send_sums(r, s):
        n, m = nd[r], 7 - nd[r]
        if s < n:
            mine = pt[r, (z - n + s + NZ + 2 * r) % NZ]
            if s > 0:
                arrived(r, 0, s - 1)
                mine = mine + rdn[r, s - 1].astype(F32)
            sdn[r, s] = mine.astype(BF)
            start(dn_copy(r, s))
        if s < m:
            mine = pt[r, (z + m - s + 2 * r) % NZ]
            if s > 0:
                arrived(r, 1, s - 1)
                mine = mine + rup[r, s - 1].astype(F32)
            sup[r, s] = mine.astype(BF)
            start(up_copy(r, s))

    def ag_copy(r, d, t, recv=False):
        t_ = t + 1 if recv else t
        c = (z + t_ + 2 * r) % NZ if d == 0 else (z - t_ + NZ + 2 * r) % NZ
        return rcopy(gb.at[r, c], gb.at[r, c], ag_s.at[r, d, t], ag_r.at[r, d, t], zdn if d == 0 else zup)

    def act(r):
        n, m = nd[r], 7 - nd[r]
        dn_copy(r, n - 1).wait_recv()
        up_copy(r, m - 1).wait_recv()
        own = (z + 2 * r) % NZ
        total = pt[r, own] + rdn[r, n - 1].astype(F32) + rup[r, m - 1].astype(F32)
        g, u, hg = total[0], total[1], total[2]
        s = jax.nn.sigmoid(g)
        silu = g * s
        gb[r, own, 2] = (silu * u).astype(BF)
        gb[r, own, 0] = (hg * u * s * (1.0 + g * (1.0 - s))).astype(BF)
        gb[r, own, 1] = (hg * silu).astype(BF)

    def spread(r, t):
        hops = (7 - nd[r], nd[r])
        for d in (0, 1):
            if 0 < t <= hops[d]:
                ag_copy(r, d, t - 1, True).wait_recv()
            if t < hops[d]:
                start(ag_copy(r, d, t))

    def stage(r, s):
        if s < 4:
            send_sums(r, s)
        else:
            if s == 4:
                act(r)
            spread(r, s - 4)

    def p0_copy(r, i):
        return rcopy(igs.at[r, 4 - 4 * core + i], igr.at[r, i], i0_s.at[r, i], i0_r.at[r, i], partner)

    def px_copy(r, n):
        m = BACK[n + 1] - 1
        return rcopy(ips.at[r, (x + DX[n]) % 4], ipr.at[r, m], ix_s.at[r, n], ix_r.at[r, m], xpeer[n])

    def px_recv(r, n):
        return rcopy(ips.at[r, 0], ipr.at[r, n], ix_s.at[r, n], ix_r.at[r, n], xpeer[n])

    def late_copy(r):
        owner = at((y + DY[r]) % 4, far[r] % 4, far[r] // 4, z)
        n = (me - far[r] + 8) % 8
        return rcopy(ils.at[r], ilr.at[n], il_s.at[r], il_r.at[n], owner)

    def late_recv(n):
        return rcopy(ils.at[0], ilr.at[n], il_s.at[0], il_r.at[n], partner)

    def input_rows(chunks):
        both = jnp.concatenate(
            [jnp.concatenate([gb[r, c, 0], gb[r, c, 1]], axis=1) for r, c in chunks], axis=0
        )
        return lax.dot_general(both, wgu[...], NT, preferred_element_type=F32).astype(BF)

    def input_early(r):
        chunks = [(r, (z + n + NZ + 2 * r) % NZ) for n in range(-3, 4)]
        part = input_rows(chunks)
        for n, (_, c) in enumerate(chunks):
            igs[r, c] = part[16 * n:16 * n + 16]
        for i in range(4):

            @pl.when(4 - 4 * core + i != far[r])
            def _(i=i):
                p0_copy(r, i).start()

    def pair_early(r):
        for n in range(4):
            i = (x + ((0,) + DX)[n]) % 4

            @pl.when(4 * core + i != far[r])
            def _(i=i, n=n):
                p0_copy(r, i).wait_recv()
                own = igs[r, 4 * core + i]
                ips[r, i] = (own.astype(F32) + igr[r, i].astype(F32)).astype(BF)
                if n > 0:
                    px_copy(r, n - 1).start()

    def input_late(*rounds):
        part = input_rows([(r, far[r]) for r in rounds])
        for n, r in enumerate(rounds):
            ils[r] = part[16 * n:16 * n + 16]
            if r > 0:
                start(late_copy(r))
            else:

                @pl.when(me != far[0])
                def _():
                    late_copy(0).start()

    def row_total(r):
        v = ips[r, x].astype(F32)
        for n in range(3):
            px_recv(r, n).wait_recv()
            v = v + ipr[r, n].astype(F32)
        return v

    def row_sum(r):
        @pl.when(me != far[r])
        def _():
            iys[r] = row_total(r).astype(BF)
            iy_copy(r).start()

    def early_end(r):
        for i in range(4):

            @pl.when(4 - 4 * core + i != far[r])
            def _(i=i):
                p0_copy(r, i).wait_send()

        for n in range(3):

            @pl.when(4 * core + (x + DX[n]) % 4 != far[r])
            def _(n=n):
                px_copy(r, n).wait_send()

        @pl.when(me != far[r])
        def _():
            if r == 0:
                late_copy(0).wait_send()
            else:
                iy_copy(r).wait_send()

    def add_dw(lhs, rhs, out):
        width = rhs.shape[1]
        for c in range(0, width, 256):
            e = min(c + 256, width)
            out[:, c:e] = jnp.dot(lhs[...], rhs[:, c:e], preferred_element_type=F32).astype(BF)

    def turn_hidden(r):
        ht[:, r * 128:r * 128 + 128] = gb[r, :, 2].reshape(128, 896).T

    def weights_part(n):
        if n < 2:
            add_dw(xt, gb[:, :, n].reshape(512, 896), (dwg_out, dwu_out)[n])
        else:
            add_dw(ht, xb[:, 1].reshape(512, 1024), dwd_out)

    def iy_copy(r):
        return rcopy(iys.at[r], iyr.at[r], iy_s.at[r], iy_r.at[r], ypeer[r])

    def finish():
        igacc[...] = jnp.zeros_like(igacc)
        for r in (3, 2, 1, 0):

            @pl.when(me != far[r])
            def _(r=r):
                if r == 0:
                    igacc[...] += row_total(0)
                else:
                    iy_copy(r).wait_recv()
                    igacc[...] += iyr[r].astype(F32)

        for r in range(4):

            @pl.when(me == far[r])
            def _(r=r):
                v = igacc[...]
                if r == 0:
                    v = v + ils[0].astype(F32)
                for n in range(1 if r == 0 else 0, 8):
                    late_recv(n).wait_recv()
                    v = v + ilr[n].astype(F32)
                igacc[...] = v

        ig_out[...] = igacc[...].astype(BF)

    marked = []

    def mark():
        marked.append(len(sends))

    def drain_marked():
        for c in sends[:marked[0]]:
            c.wait_send()
        del sends[:marked[0]]

    def drain():
        for c in sends:
            c.wait_send()
        sends.clear()
        for r in range(4):
            early_end(r)

    steps = []

    def then(fn, *given):
        steps.append((fn, given))

    then(own_sends)
    then(row_in, 0)
    then(row_in, 1)
    then(partials, 0)
    then(third_in, 0)
    then(third_in, 1)
    then(hand_over, 1)
    then(partials, 1)
    then(hand_over, 2)
    then(stage, 0, 1)
    then(partials, 2)
    then(hand_over, 3)
    then(partials, 3)
    then(mark)
    then(stage, 1, 1)
    then(stage, 0, 2)
    then(stage, 2, 1)
    done, last = [2, 1, 1, 0], [0, 2]
    while min(done) < 6:
        free = [q for q in (3, 2, 1, 0) if q not in last[-2:] and done[q] < 6]
        r = min(free or (3, 2, 1, 0), key=lambda q: done[q])
        done[r] += 1
        last.append(r)
        then(stage, r, done[r])
    then(drain_marked)
    then(stage, 3, 7)
    then(input_early, 3)
    then(stage, 2, 7)
    then(input_early, 2)
    then(pair_early, 3)
    then(stage, 1, 7)
    then(input_early, 1)
    then(pair_early, 2)
    then(stage, 0, 7)
    then(input_early, 0)
    then(pair_early, 1)
    then(stage, 3, 8)
    then(stage, 2, 8)
    then(input_late, 3, 2)
    then(pair_early, 0)
    then(stage, 1, 8)
    then(stage, 0, 8)
    then(input_late, 1, 0)
    for r in range(4):
        then(turn_hidden, r)
    then(row_sum, 3)
    then(row_sum, 2)
    then(row_sum, 1)
    for n in range(3):
        then(weights_part, n)
    then(drain)
    then(finish)
    for fn, given in steps:
        fn(*given)


def writer(*refs):
    sem = refs[8]
    copies = [pltpu.make_async_copy(refs[i], refs[4 + i], sem.at[i]) for i in range(4)]
    for c in copies:
        c.start()
    for c in copies:
        c.wait()


def local(tokens_in, cotangent, gate_weight, up_weight, down_weight):
    vm = pltpu.VMEM
    dma = pltpu.SemaphoreType.DMA
    outs = pl.pallas_call(
        kernel,
        out_shape=(
            pltpu.VMEM((16, 1024), BF),
            pltpu.VMEM((1024, 896), BF),
            pltpu.VMEM((1024, 896), BF),
            pltpu.VMEM((896, 1024), BF),
        ),
        in_specs=[pl.BlockSpec(memory_space=pl.ANY)] * 5,
        out_specs=[pl.BlockSpec(memory_space=pltpu.VMEM)] * 4,
        scratch_shapes=[
            vm((4, 2, 8, 16, 1024), BF),
            vm((1024, 512), BF),
            vm((896, 512), BF),
            vm((1024, 1792), BF),
            vm((896, 1024), BF),
            vm((4, 8, 3, 16, 896), F32),
            vm((4, 4, 3, 16, 896), BF),
            vm((4, 4, 3, 16, 896), BF),
            vm((4, 4, 3, 16, 896), BF),
            vm((4, 4, 3, 16, 896), BF),
            vm((4, 8, 3, 16, 896), BF),
            vm((4, 8, 16, 1024), BF),
            vm((4, 4, 16, 1024), BF),
            vm((4, 4, 16, 1024), BF),
            vm((4, 3, 16, 1024), BF),
            vm((4, 16, 1024), BF),
            vm((8, 16, 1024), BF),
            vm((4, 16, 1024), BF),
            vm((4, 16, 1024), BF),
            vm((16, 1024), F32),
            dma((5,)),
            dma((4, 2, 4)), dma((4, 2, 4)),
            dma((4, 2, 4)), dma((4, 2, 4)),
            dma((2, 2)), dma((2, 2)),
            dma((4, 2, 4)), dma((4, 2, 4)),
            dma((4, 2, 4)), dma((4, 2, 4)),
            dma((4, 4)), dma((4, 4)),
            dma((4, 3)), dma((4, 3)),
            dma((4,)), dma((8,)),
            dma((4,)), dma((4,)),
        ],
        compiler_params=pltpu.CompilerParams(
            collective_id=0, has_side_effects=True, vmem_limit_bytes=48 * 2**20
        ),
        cost_estimate=pl.CostEstimate(flops=7_516_000_000, bytes_accessed=11_000_000, transcendentals=0),
    )(tokens_in, cotangent, gate_weight, up_weight, down_weight)
    outs = [pltpu.with_memory_space_constraint(a, pltpu.MemorySpace.VMEM) for a in outs]
    return pl.pallas_call(
        writer,
        out_shape=(
            jax.ShapeDtypeStruct((16, 1024), BF),
            jax.ShapeDtypeStruct((1024, 896), BF),
            jax.ShapeDtypeStruct((1024, 896), BF),
            jax.ShapeDtypeStruct((896, 1024), BF),
        ),
        in_specs=[pl.BlockSpec(memory_space=pltpu.VMEM)] * 4,
        out_specs=[pl.BlockSpec(memory_space=pl.ANY)] * 4,
        scratch_shapes=[pltpu.SemaphoreType.DMA((4,))],
        compiler_params=pltpu.CompilerParams(vmem_limit_bytes=2**20),
        cost_estimate=pl.CostEstimate(flops=0, bytes_accessed=11_000_000, transcendentals=0),
    )(*outs)


def solution(mesh):
    in_specs = (
        P(("tok", "fout"), "fin"),
        P(("tok", "fout"), "fin"),
        P("fin", ("tok", "fout")),
        P("fin", ("tok", "fout")),
        P(("tok", "fout"), "fin"),
    )
    out_specs = (
        P(("tok", "fout"), "fin"),
        P("fin", ("tok", "fout")),
        P("fin", ("tok", "fout")),
        P(("tok", "fout"), "fin"),
    )
    return jax.shard_map(local, mesh=mesh, in_specs=in_specs, out_specs=out_specs, check_vma=False)
```
